128 devices in a mesh: rep: 16 (over x, z), tp: 8 (over y, core).
Axes of the slice: x: 4, y: 4, z: 4, core: 2. Of those that a mesh axis runs over, the one named last changes fastest.
Arguments:
- normed_hidden_input: bfloat16 [3, 2048, 8192], P(None, 'rep', 'tp'), may hold values from -6 to 6
- query_key_value_weight: bfloat16 [8192, 8, 1280], P(None, 'tp'), may hold values from -0.0625 to 0.0625
- adapter_down_weight: bfloat16 [128, 8192, 64], P('rep', 'tp'), may hold values from -0.0625 to 0.0625
- adapter_up_weight: bfloat16 [128, 64, 8, 1280], P('rep', None, 'tp'), may hold values from -0.75 to 0.75
- cached_rotated_keys: bfloat16 [2048, 8, 128, 128], P('rep', 'tp'), may hold values from -1000 to 1000
- cached_value_rows: bfloat16 [2048, 8, 128, 128], P('rep', 'tp'), may hold values from -6 to 6
- cached_length_valid: int32 [2048], P('rep'), may hold values from 2 to 128, as said below
- request_adapter: int32 [2048], P('rep'), may hold values from 0 to 127, as said below
- adapter_storage_slot: int32 [128], replicated, may hold values from 0 to 127, as said below
Outputs:
- attended: bfloat16 [3, 2048, 8192], P(None, 'rep', 'tp')
The draws below stay inside these ranges and needn't reach their ends.
Inputs may be any that keep to these rules, and one draw needn't show every extreme that they name: `adapter_storage_slot`: each slot is used once; slots s * 8 to (s + 1) * 8 - 1 are stored on replica s. `request_adapter`: among the 128 requests of one replica, at most 32 use adapters stored on any one replica; in every draw some replica stores the adapters of exactly 32 requests of every replica. `cached_length_valid`: every replica has a request with 128 cached positions.
All inputs are finite; a program needn't handle non-finite values.
Results may differ from the reference program's by a relative error of at most 0.015.
Values may be sent and summed in bfloat16 or wider, within the bound.
A program may use at most 192 MiB of HBM per device.

```python
import jax
import jax.numpy as jnp
from jax import lax

MODEL_WIDTH = 8192
HEADS = 64
KEY_VALUE_HEADS = 8
HEAD_DIM = 128
ADAPTER_RANK = 64
STEPS = 3
REQUEST_ROWS = 128
CACHE = 128
ADP_REP = 8
GROUP = 8
JOINED_COLUMNS = 1280
ADAPTER_TOTAL = 128
ROWS_ALL = 2048
MOST = 32
N_REP = 16


def slot_table(key):
    return jax.random.permutation(key, ADAPTER_TOTAL).astype(jnp.int32)


def draw_adapter_storage_slot(key, part):
    table = slot_table(key)
    return table


def draw_request_adapter(key, part):
    table = slot_table(key)
    key = jax.random.fold_in(key, 7)
    keys = jax.random.split(key, 4)
    hottest = jax.random.randint(keys[0], (), 0, N_REP)
    others = jax.vmap(lambda single: jax.random.permutation(single, N_REP - 1))(jax.random.split(keys[1], N_REP))
    others = (hottest + 1 + others) % N_REP
    spread = jnp.arange(REQUEST_ROWS - MOST) % (N_REP - 1)
    remaining = others[:, spread].astype(jnp.int32)
    owners = jnp.concatenate([jnp.full((N_REP, MOST), hottest, jnp.int32), remaining], axis=1)
    shuffle = jax.vmap(lambda single: jax.random.permutation(single, REQUEST_ROWS))(jax.random.split(keys[2], N_REP))
    owners = jnp.take_along_axis(owners, shuffle, axis=1)
    within = jax.random.randint(keys[3], (N_REP, REQUEST_ROWS), 0, ADP_REP)
    slots = (owners * ADP_REP + within).reshape(ROWS_ALL)
    inverse = jnp.zeros((ADAPTER_TOTAL,), jnp.int32).at[table].set(jnp.arange(ADAPTER_TOTAL, dtype=jnp.int32))
    return inverse[slots]


def draw_cached_length_valid(key, part):
    key = jax.random.fold_in(key, 11)
    keys = jax.random.split(key, 2)
    lengths = jax.random.randint(keys[0], (N_REP, REQUEST_ROWS), 2, CACHE + 1)
    chosen = jax.random.randint(keys[1], (N_REP,), 0, REQUEST_ROWS)
    lengths = jnp.where(jnp.arange(REQUEST_ROWS)[None, :] == chosen[:, None], CACHE, lengths)
    return lengths.reshape(ROWS_ALL).astype(jnp.int32)


def draw_cached_rotated_keys(key, part):
    key = jax.random.fold_in(key, 13)
    keys = jax.random.split(key, 1)
    array_shape = (ROWS_ALL, KEY_VALUE_HEADS, CACHE, HEAD_DIM)
    values = jnp.clip(jax.random.normal(keys[0], array_shape, jnp.float32), -6.0, 6.0)
    return values.astype(jnp.bfloat16)


def shard_levels(rng, dims, shards, smallest, largest):
    def one(axis_at, parts):
        steps = jax.random.uniform(jax.random.fold_in(jax.random.fold_in(rng, 6), axis_at), (parts,), jnp.float32, smallest / len(shards), largest / len(shards))
        return jnp.repeat(jnp.exp(steps), dims[axis_at] // parts).reshape((-1,) + (1,) * (len(dims) - axis_at - 1))

    gain = one(*shards[0])
    for cut in shards[1:]:
        gain = gain * one(*cut)
    return gain


def bell_draw(key, shape, deviation, most, shards=(), held_as=jnp.bfloat16):
    level = shard_levels(key, shape, shards, -0.22, 0.18) if shards else 1.0
    result = jax.random.normal(key, shape, jnp.float32) * deviation * level
    return jnp.minimum(jnp.maximum(result, -most), most).astype(held_as)


def setup_inputs(seed: int = 0) -> dict:
    streams_of = jax.random.split(jax.random.key(seed), 10)
    return {
        "normed_hidden_input": bell_draw(streams_of[0], (STEPS, ROWS_ALL, MODEL_WIDTH), 1.0, 6.0, ((1, 16), (2, 8))),
        "query_key_value_weight": bell_draw(streams_of[1], (MODEL_WIDTH, KEY_VALUE_HEADS, JOINED_COLUMNS), MODEL_WIDTH ** -0.5, 0.0625, ((1, 8),)),
        "adapter_down_weight": bell_draw(streams_of[2], (ADAPTER_TOTAL, MODEL_WIDTH, ADAPTER_RANK), MODEL_WIDTH ** -0.5, 0.0625, ((0, 16), (1, 8))),
        "adapter_up_weight": bell_draw(streams_of[3], (ADAPTER_TOTAL, ADAPTER_RANK, KEY_VALUE_HEADS, JOINED_COLUMNS), ADAPTER_RANK ** -0.5, 0.75, ((0, 16), (2, 8))),
        "cached_rotated_keys": draw_cached_rotated_keys(jax.random.fold_in(streams_of[9], 71), 0),
        "cached_value_rows": bell_draw(streams_of[5], (ROWS_ALL, KEY_VALUE_HEADS, CACHE, HEAD_DIM), 1.0, 6.0, ((0, 16), (1, 8))),
        "cached_length_valid": draw_cached_length_valid(jax.random.fold_in(streams_of[9], 71), 0),
        "request_adapter": draw_request_adapter(jax.random.fold_in(streams_of[9], 71), 0),
        "adapter_storage_slot": draw_adapter_storage_slot(jax.random.fold_in(streams_of[9], 71), 0),
    }


def rotate(vector, position):
    half = vector.shape[-1] // 2
    freqs = jnp.exp(jnp.arange(half, dtype=jnp.float32) * (-2.0 / vector.shape[-1]) * jnp.log(jnp.float32(500000.0)))
    angle = position[:, None] * freqs[None, :]
    target = (position.shape[0],) + (1,) * (vector.ndim - 2) + (half,)
    cosine = jnp.cos(angle).reshape(target)
    sine = jnp.sin(angle).reshape(target)
    first = vector[..., :half]
    second = vector[..., half:]
    return jnp.concatenate([first * cosine - second * sine, second * cosine + first * sine], axis=-1)


def adapter_update(hidden_state, storage_slot_rows, adapter_down_weight, adapter_up_weight):
    blocks = hidden_state.reshape(N_REP, REQUEST_ROWS, MODEL_WIDTH)
    slot_blocks = storage_slot_rows.reshape(N_REP, REQUEST_ROWS)

    def one_block(operands):
        block_rows, block_slot_index = operands
        down_projected_rows = adapter_down_weight[block_slot_index].astype(jnp.float32)
        low = jnp.einsum("rd,rdk->rk", block_rows.astype(jnp.float32), down_projected_rows)
        low = lax.optimization_barrier(low.astype(jnp.bfloat16)).astype(jnp.float32)
        up_projected_rows = adapter_up_weight[block_slot_index].astype(jnp.float32).reshape(REQUEST_ROWS, ADAPTER_RANK, KEY_VALUE_HEADS * JOINED_COLUMNS)
        return jnp.einsum("rk,rkc->rc", low, up_projected_rows).astype(jnp.bfloat16)

    return lax.map(one_block, (blocks, slot_blocks)).reshape(ROWS_ALL, KEY_VALUE_HEADS * JOINED_COLUMNS)


def attend(query, cached_rotated_keys, cached_value_rows, fresh_keys, fresh_values, cached_length_valid):
    factor = HEAD_DIM ** -0.5
    cache_scores = jnp.einsum("rhgd,rhpd->rhgp", query.astype(jnp.float32), cached_rotated_keys.astype(jnp.float32)) * factor
    valid = jnp.arange(CACHE, dtype=jnp.int32)[None, :] < cached_length_valid[:, None]
    cache_scores = jnp.where(valid[:, None, None, :], cache_scores, -jnp.inf)
    fresh_scores = jnp.einsum("rhgd,rhjd->rhgj", query.astype(jnp.float32), fresh_keys.astype(jnp.float32)) * factor
    highest = jnp.maximum(jnp.max(cache_scores, axis=-1), jnp.max(fresh_scores, axis=-1))[..., None]
    cache_exp = jnp.exp(cache_scores - highest)
    fresh_exp = jnp.exp(fresh_scores - highest)
    denominator = jnp.sum(cache_exp, axis=-1, keepdims=True) + jnp.sum(fresh_exp, axis=-1, keepdims=True)
    cache_weights = (cache_exp / denominator).astype(jnp.bfloat16)
    fresh_weights = (fresh_exp / denominator).astype(jnp.bfloat16)
    mixed = jnp.einsum("rhgp,rhpd->rhgd", cache_weights.astype(jnp.float32), cached_value_rows.astype(jnp.float32))
    mixed = mixed + jnp.einsum("rhgj,rhjd->rhgd", fresh_weights.astype(jnp.float32), fresh_values.astype(jnp.float32))
    return mixed.astype(jnp.bfloat16)


def reference(normed_hidden_input, query_key_value_weight, adapter_down_weight, adapter_up_weight, cached_rotated_keys, cached_value_rows, cached_length_valid, request_adapter, adapter_storage_slot):
    storage_slot_rows = adapter_storage_slot[request_adapter]
    weight = query_key_value_weight.reshape(MODEL_WIDTH, KEY_VALUE_HEADS * JOINED_COLUMNS)
    query_width = GROUP * HEAD_DIM
    fresh_key_list = []
    fresh_value_list = []
    results = []
    for step in range(STEPS):
        decode_step_rows = normed_hidden_input[step]
        joined = jnp.dot(decode_step_rows, weight, preferred_element_type=jnp.float32)
        update_term = lax.optimization_barrier(adapter_update(decode_step_rows, storage_slot_rows, adapter_down_weight, adapter_up_weight))
        joined = (joined + update_term.astype(jnp.float32)).reshape(ROWS_ALL, KEY_VALUE_HEADS, JOINED_COLUMNS)
        position = cached_length_valid.astype(jnp.float32) + step
        query = rotate(joined[..., :query_width].reshape(ROWS_ALL, KEY_VALUE_HEADS, GROUP, HEAD_DIM), position).astype(jnp.bfloat16)
        fresh_key_list.append(rotate(joined[..., query_width:query_width + HEAD_DIM], position).astype(jnp.bfloat16))
        fresh_value_list.append(joined[..., query_width + HEAD_DIM:].astype(jnp.bfloat16))
        mixed = attend(query, cached_rotated_keys, cached_value_rows, jnp.stack(fresh_key_list, 2), jnp.stack(fresh_value_list, 2), cached_length_valid)
        results.append(mixed.reshape(ROWS_ALL, HEADS * HEAD_DIM))
    return jnp.stack(results)
```

```python
import functools

import jax
import jax.numpy as jnp
import numpy as np
from jax import lax
from jax.experimental import pallas as pl
from jax.experimental.pallas import tpu as pltpu
from jax.sharding import PartitionSpec as P

MESH = pl.DeviceIdType.MESH
F32 = jnp.float32
BF16 = jnp.bfloat16
STEPS = 3
REQS = 128
ROWS = STEPS * REQS
WIDTH = 1024
OUT = 1280
RANKS = 512
CHUNK = 256
CHUNKS = OUT // CHUNK
HALF = ROWS // 2
PACK = ROWS // 2
PART = PACK // 8
PARTPAD = 32
QROWS = 24


def dot(a, b):
    return jnp.dot(a, b, preferred_element_type=F32)


def dot_nt(a, b):
    return lax.dot_general(a, b, (((1,), (1,)), ((), ())), preferred_element_type=F32)


def column(row):
    return jnp.transpose(jnp.broadcast_to(row, (128, 128)))


def project(
    hid,
    weight,
    down,
    up,
    req_ref,
    table_ref,
    len_ref,
    query_out,
    key_out,
    value_out,
    xs,
    rows,
    downs,
    ups,
    wbuf,
    base,
    spread,
    acc,
    reqs,
    slots,
    cosine,
    sine,
    home,
    home_in,
    part_in,
    low_part,
    low_parts,
    low_own,
    lows,
    dsend,
    relay_in,
    back_in,
    ssem,
    rsem,
    lsem,
):
    rep = lax.axis_index("rep")
    tp = lax.axis_index("tp")
    x, z, y, c = rep // 4, rep % 4, tp // 2, tp % 2
    r = z * (1 - c) + x * c
    w = x * (1 - c) + z * c

    def rep_at(r_, w_):
        return (w_ * (1 - c) + r_ * c) * 4 + r_ * (1 - c) + w_ * c

    def dev(rep_, tp_):
        return {"rep": rep_, "tp": tp_}

    shift = (0, 3, 1, 2)
    row_reps = [rep_at((r + s) % 4, w) for s in shift]
    weight_reps = [rep_at(r, (w + s) % 4) for s in shift]
    row_dev = [dev(q, tp) for q in row_reps]
    weight_dev = [dev(q, tp) for q in weight_reps]
    tps = [((y + s) % 4) * 2 + c for s in shift]
    sib_tps = [((y + s) % 4) * 2 + 1 - c for s in shift]
    y_dev = [dev(rep, q) for q in tps]
    sibling = dev(rep, sib_tps[0])
    tp_dev = [dev(rep, (tp + k) % 8) for k in range(8)]

    count = [0]

    def remote(src, dst, device):
        i = count[0]
        count[0] += 1
        return pltpu.make_async_remote_copy(
            src_ref=src,
            dst_ref=dst,
            send_sem=ssem.at[i],
            recv_sem=rsem.at[i],
            device_id=device,
            device_id_type=MESH,
        )

    lcount = [0]

    def local(src, dst):
        i = lcount[0]
        lcount[0] += 1
        return pltpu.make_async_copy(src, dst, lsem.at[i])

    sent = []

    def go(*copies):
        for cp in copies:
            cp.start()
            sent.append(cp)

    class Ring:
        def __init__(self, src, slot, size, devs):
            a, b = pl.ds(0, size // 2), pl.ds(size // 2, size // 2)
            left, right = devs[1], devs[2]
            self.first = [
                remote(src(a), slot(1, a), right),
                remote(src(b), slot(2, b), left),
            ]
            self.second = [
                remote(src(b), slot(1, b), right),
                remote(src(a), slot(2, a), left),
            ]
            self.far = [
                remote(slot(1, a), slot(3, a), right),
                remote(slot(2, b), slot(3, b), left),
            ]

        def relay(self):
            for i in range(2):
                self.first[i].wait_recv()
                go(self.far[i])

        def near(self):
            for i in range(2):
                self.second[i].wait_recv()

        def rest(self):
            for i in range(2):
                self.far[i].wait_recv()

    load_rows = local(hid, rows.at[0])
    load_down = local(down, downs.at[0])
    load_up = local(up, ups.at[0])
    order = [(i, s) for i in range(4) for s in range(2)]
    load_w = []
    for i, s in order:
        t_ = (tps if s == 0 else sib_tps)[i]
        load_w.append(
            local(weight.at[pl.ds(pl.multiple_of(t_ * WIDTH, WIDTH), WIDTH), :], wbuf.at[i * 2 + s])
        )
    load_rows.start()
    load_down.start()
    load_w[0].start()
    load_w[1].start()

    reqs[0] = jnp.broadcast_to(req_ref[...], (8, 128))

    barrier = pltpu.get_barrier_semaphore()
    peers = [row_dev[1], row_dev[2], row_dev[3], weight_dev[1], weight_dev[2]] + tp_dev[1:]
    for peer in peers:
        pl.semaphore_signal(barrier, inc=1, device_id=peer, device_id_type=MESH)
    pl.semaphore_wait(barrier, len(peers))

    y_ring = Ring(lambda h: hid.at[h], lambda s, h: xs.at[2 * s, h], ROWS, y_dev)
    r_ring = Ring(lambda h: hid.at[h], lambda s, h: rows.at[s, h], ROWS, row_dev)
    w_ring = Ring(lambda h: down.at[h], lambda s, h: downs.at[s, h], RANKS, weight_dev)
    up_rings = []
    for k in range(CHUNKS):
        cols = pl.ds(k * CHUNK, CHUNK)
        up_rings.append(
            Ring(
                lambda h, cols=cols: up.at[h, cols],
                lambda s, h, cols=cols: ups.at[s, h, cols],
                RANKS,
                weight_dev,
            )
        )
    req_copies = [remote(reqs.at[0], reqs.at[(0, 2, 1, 3)[i]], row_dev[i]) for i in (1, 2, 3)]
    sib_copies = [remote(hid, xs.at[1], sibling)] + [
        remote(xs.at[2 * i], xs.at[2 * i + 1], sibling) for i in (1, 2, 3)
    ]

    go(*req_copies)
    go(*w_ring.first, *r_ring.first, *y_ring.first)
    go(*w_ring.second, *r_ring.second, *y_ring.second)
    go(sib_copies[0])
    for cp in load_w[2:]:
        cp.start()
    load_up.start()

    lane = lax.broadcasted_iota(jnp.int32, (128, 128), 1)
    low_lane = lane < 64

    freq = jnp.exp((lane % 64).astype(F32) * (-2.0 / 128) * jnp.log(F32(500000.0)))
    pos = column(len_ref[...]).astype(F32)
    for t in range(STEPS):
        angle = (pos + t) * freq
        part = pl.ds(t * REQS, REQS)
        cosine[part, :] = jnp.cos(angle)
        sine[part, :] = jnp.where(low_lane, -1.0, 1.0) * jnp.sin(angle)

    def rotate(v):
        return v * cosine[...] + pltpu.roll(v, 64, 1) * sine[...]

    def find_slots(i):
        hit = column(reqs[i, 0:1, :]) == lane
        found = jnp.sum(
            jnp.where(hit, jnp.broadcast_to(table_ref[...], (128, 128)), 0).astype(F32),
            axis=1,
            keepdims=True,
        )
        slots[i] = jnp.broadcast_to(found, (128, 128)).astype(jnp.int32)

    find_slots(0)

    def base_mm(x_ref, j, first=False):
        load_w[j].wait()

        @pl.loop(0, CHUNKS)
        def _(n):
            cols = pl.ds(pl.multiple_of(n * CHUNK, CHUNK), CHUNK)
            got = dot(x_ref[...], wbuf[j, :, cols])
            if first:
                base[:, cols] = got
            else:
                base[:, cols] += got

    def down_mm(i, j):
        @pl.loop(0, 2)
        def _(h):
            part = pl.ds(pl.multiple_of(h * 256, 256), 256)
            got = dot_nt(rows[i], downs[j, part, :])
            for p in range(2):
                target = weight_reps[j] * 8 + h * 4 + 2 * p + jnp.where(low_lane, 0, 1)
                hit = slots[i] == target
                for t in range(STEPS):
                    tt = pl.ds(t * REQS, REQS)
                    acc[i, tt, :] += jnp.where(
                        hit, got[t * REQS : (t + 1) * REQS, p * 128 : (p + 1) * 128], 0.0
                    )

    acc[...] = jnp.zeros_like(acc)
    load_rows.wait()
    base_mm(rows.at[0], 0, first=True)
    load_down.wait()
    down_mm(0, 0)
    for cp in req_copies:
        cp.wait_recv()
    for i in (1, 2, 3):
        find_slots(i)
    sib_copies[0].wait_recv()
    base_mm(xs.at[1], 1)

    y_ring.relay()
    r_ring.relay()
    w_ring.relay()

    y_ring.near()
    go(sib_copies[1], sib_copies[2])
    r_ring.near()
    down_mm(1, 0)
    down_mm(2, 0)
    base_mm(xs.at[2], 2)
    w_ring.near()
    go(*up_rings[0].first, *up_rings[0].second)
    for j in (1, 2):
        for i in (0, 1, 2):
            down_mm(i, j)
    y_ring.rest()
    go(sib_copies[3])
    r_ring.rest()
    for j in (0, 1, 2):
        down_mm(3, j)
    w_ring.rest()
    go(*up_rings[1].first, *up_rings[1].second)
    go(*up_rings[2].first, *up_rings[2].second)
    for i in (3, 1, 2, 0):
        down_mm(i, 3)

    home_copies = []
    for i in range(4):
        both = acc[i] + pltpu.roll(acc[i], 64, 1)
        lane_h = lax.broadcasted_iota(jnp.int32, (PACK, 128), 1) < 64
        home[i] = jnp.where(lane_h, both[:PACK], both[PACK:])
        if i:
            cp = remote(home.at[i], home_in.at[(0, 2, 1, 3)[i]], row_dev[i])
            home_copies.append(cp)
            go(cp)
    up_rings[0].relay()
    for cp in home_copies:
        cp.wait_recv()
    home[0] = (home[0] + home_in[1]) + (home_in[2] + home_in[3])
    part_copies = []
    for k in range(1, 8):
        target = (tp + k) % 8
        cp = remote(
            home.at[0, pl.ds(pl.multiple_of(target * PART, 8), PART), :], part_in.at[k], tp_dev[k]
        )
        part_copies.append(cp)
        go(cp)
    go(*up_rings[3].first, *up_rings[3].second)
    up_rings[1].relay()
    for i in (1, 2):
        sib_copies[i].wait_recv()
    base_mm(xs.at[4], 4)
    for cp in part_copies:
        cp.wait_recv()
    total = home[0, pl.ds(pl.multiple_of(tp * PART, 8), PART), :]
    for k in range(1, 8):
        total = total + part_in[k]
    low_part[...] = jnp.concatenate([total, jnp.zeros((PARTPAD - PART, 128), F32)], 0).astype(BF16)
    low_copies = []
    for k in range(1, 8):
        cp = remote(low_part, low_parts.at[k], tp_dev[k])
        low_copies.append(cp)
        go(cp)
    go(*up_rings[4].first, *up_rings[4].second)
    up_rings[2].relay()
    base_mm(xs.at[3], 3)
    for cp in low_copies:
        cp.wait_recv()
    low_own[pl.ds(pl.multiple_of(tp * PART, 8), PART), :] = low_part[...].astype(F32)[:PART]
    for k in range(1, 8):
        source = (tp + 8 - k) % 8
        low_own[pl.ds(pl.multiple_of(source * PART, 8), PART), :] = low_parts[k].astype(F32)[:PART]
    lows[0] = low_own[...].astype(BF16)
    back_low = [remote(lows.at[0], lows.at[(0, 2, 1, 3)[i]], row_dev[i]) for i in (1, 2, 3)]
    go(*back_low)

    def spread_rows(i):
        packed = lows[i].astype(F32)
        turned = pltpu.roll(packed, 64, 1)
        lane_h = lax.broadcasted_iota(jnp.int32, (PACK, 128), 1) < 64
        low = jnp.concatenate(
            [jnp.where(lane_h, packed, turned), jnp.where(lane_h, turned, packed)], 0
        )
        for j in range(4):
            for p in range(4):
                target = weight_reps[j] * 8 + 2 * p + jnp.where(low_lane, 0, 1)
                hit = slots[i] == target
                for t in range(STEPS):
                    tt = slice(t * REQS, (t + 1) * REQS)
                    spread[i, tt, (j * 4 + p) * 128 : (j * 4 + p + 1) * 128] = jnp.where(
                        hit, low[tt], 0.0
                    ).astype(BF16)

    spread_rows(0)
    up_rings[3].relay()
    base_mm(xs.at[5], 5)
    for cp in back_low:
        cp.wait_recv()
    for i in (3, 1, 2):
        spread_rows(i)
    load_up.wait()

    order_c = (4, 0, 1, 2, 3)

    def delta(i, k):
        total = None
        for j in range(4):
            got = dot(spread[i, :, j * RANKS : (j + 1) * RANKS], ups[j, :, k * CHUNK : (k + 1) * CHUNK])
            total = got if total is None else total + got
        dsend[i, k] = total.astype(BF16)

    ha, hb = pl.ds(0, HALF), pl.ds(HALF, HALF)
    far_back, near_back, late_back = {}, {}, {}

    def send_chunk(k):
        up_rings[k].near()
        up_rings[k].rest()
        delta(3, k)
        far_back[k] = [
            remote(dsend.at[3, k, ha], relay_in.at[0, k], row_dev[2]),
            remote(dsend.at[3, k, hb], relay_in.at[1, k], row_dev[1]),
        ]
        go(*far_back[k])
        delta(1, k)
        delta(2, k)
        near_back[k] = [
            remote(dsend.at[2, k, hb], back_in.at[0, k, hb], row_dev[2]),
            remote(dsend.at[1, k, ha], back_in.at[1, k, ha], row_dev[1]),
        ]
        go(*near_back[k])
        delta(0, k)

    def relay_chunk(k):
        far_back[k][0].wait_recv()
        dsend[2, k, ha, :] = dsend[2, k, ha, :] + relay_in[0, k]
        far_back[k][1].wait_recv()
        dsend[1, k, hb, :] = dsend[1, k, hb, :] + relay_in[1, k]
        late_back[k] = [
            remote(dsend.at[2, k, ha], back_in.at[0, k, ha], row_dev[2]),
            remote(dsend.at[1, k, hb], back_in.at[1, k, hb], row_dev[1]),
        ]
        go(*late_back[k])

    def finish_chunk(k):
        for cp in near_back[k] + late_back[k]:
            cp.wait_recv()
        add = (dsend[0, k].astype(F32) + back_in[0, k].astype(F32)) + back_in[1, k].astype(F32)
        joined = base[:, k * CHUNK : (k + 1) * CHUNK] + add
        if k == CHUNKS - 1:
            key = rotate(joined[:, :128])
            for t in range(STEPS):
                tt = slice(t * REQS, (t + 1) * REQS)
                key_out[pl.ds(t, REQS, stride=8), :] = key[tt]
                value_out[pl.ds(t, REQS, stride=8), :] = joined[tt, 128:]
        else:
            for g in range(2):
                query = rotate(joined[:, g * 128 : (g + 1) * 128])
                for t in range(STEPS):
                    tt = slice(t * REQS, (t + 1) * REQS)
                    query_out[pl.ds(t * 8 + 2 * k + g, REQS, stride=QROWS), :] = query[tt]

    key_out[...] = jnp.zeros_like(key_out)
    value_out[...] = jnp.zeros_like(value_out)
    o = (0, 1, 2, 3, 4)
    up_rings[4].relay()
    send_chunk(o[0])
    send_chunk(o[1])
    sib_copies[3].wait_recv()
    base_mm(xs.at[6], 6)
    base_mm(xs.at[7], 7)
    relay_chunk(o[0])
    send_chunk(o[2])
    relay_chunk(o[1])
    finish_chunk(o[0])
    send_chunk(o[3])
    relay_chunk(o[2])
    finish_chunk(o[1])
    send_chunk(o[4])
    relay_chunk(o[3])
    finish_chunk(o[2])
    relay_chunk(o[4])
    finish_chunk(o[3])
    finish_chunk(o[4])
    for cp in sent:
        cp.wait_send()


BLOCK = 16


def attend(lens, query, key, value, keys, values, out, mixed, scores):
    step = pl.program_id(0)
    rows = BLOCK * QROWS
    factor = 128**-0.5
    q = query[...].astype(BF16)
    row = lax.broadcasted_iota(jnp.int32, (rows, 128), 0)
    lane = lax.broadcasted_iota(jnp.int32, (rows, 128), 1)
    fresh = dot_nt(q, key[...].astype(BF16)) * factor
    open_ = (row // QROWS == lane // 8) & (lane % 8 <= (row % QROWS) // 8)
    fresh = jnp.where(open_, fresh, -jnp.inf)
    lane_q = lax.broadcasted_iota(jnp.int32, (QROWS, 128), 1)
    for i in range(BLOCK):
        part = pl.ds(i * QROWS, QROWS)
        got = dot_nt(q[i * QROWS : (i + 1) * QROWS], keys[i]) * factor
        scores[part, :] = jnp.where(lane_q < lens[step * BLOCK + i], got, -jnp.inf)
    cached = scores[...]
    highest = jnp.max(jnp.maximum(cached, fresh), axis=1, keepdims=True)
    cached = jnp.exp(cached - highest)
    fresh = jnp.exp(fresh - highest)
    total = jnp.sum(cached + fresh, axis=1, keepdims=True)
    cached = (cached / total).astype(BF16)
    fresh = (fresh / total).astype(BF16)
    mixed[...] = dot(fresh, value[...].astype(BF16))
    for i in range(BLOCK):
        part = pl.ds(i * QROWS, QROWS)
        mixed[part, :] += dot(cached[i * QROWS : (i + 1) * QROWS], values[i])
    for t in range(STEPS):
        for g in range(8):
            out[t, :, g * 128 : (g + 1) * 128] = mixed[
                pl.ds(t * 8 + g, BLOCK, stride=QROWS), :
            ].astype(BF16)


def local(
    normed_hidden_input,
    query_key_value_weight,
    adapter_down_weight,
    adapter_up_weight,
    cached_rotated_keys,
    cached_value_rows,
    cached_length_valid,
    request_adapter,
    adapter_storage_slot,
):
    hid = normed_hidden_input.reshape(ROWS, WIDTH)
    weight = query_key_value_weight.reshape(8 * WIDTH, OUT)
    down = jnp.swapaxes(adapter_down_weight, 1, 2).reshape(RANKS, WIDTH)
    up = adapter_up_weight.reshape(RANKS, OUT)
    anywhere = pl.BlockSpec(memory_space=pl.ANY)
    in_vmem = pl.BlockSpec(memory_space=pltpu.VMEM)
    copies = 140
    query, key, value = pl.pallas_call(
        project,
        out_shape=(
            jax.ShapeDtypeStruct((REQS * QROWS, 128), F32),
            jax.ShapeDtypeStruct((REQS * 8, 128), F32),
            jax.ShapeDtypeStruct((REQS * 8, 128), F32),
        ),
        in_specs=[anywhere] * 4 + [in_vmem] * 3,
        out_specs=(in_vmem, in_vmem, in_vmem),
        scratch_shapes=[
            pltpu.VMEM((8, ROWS, WIDTH), BF16),
            pltpu.VMEM((4, ROWS, WIDTH), BF16),
            pltpu.VMEM((4, RANKS, WIDTH), BF16),
            pltpu.VMEM((4, RANKS, OUT), BF16),
            pltpu.VMEM((8, WIDTH, OUT), BF16),
            pltpu.VMEM((ROWS, OUT), F32),
            pltpu.VMEM((4, ROWS, 4 * RANKS), BF16),
            pltpu.VMEM((4, ROWS, 128), F32),
            pltpu.VMEM((4, 8, 128), jnp.int32),
            pltpu.VMEM((4, 128, 128), jnp.int32),
            pltpu.VMEM((ROWS, 128), F32),
            pltpu.VMEM((ROWS, 128), F32),
            pltpu.VMEM((4, PACK, 128), F32),
            pltpu.VMEM((4, PACK, 128), F32),
            pltpu.VMEM((8, PART, 128), F32),
            pltpu.VMEM((PARTPAD, 128), BF16),
            pltpu.VMEM((8, PARTPAD, 128), BF16),
            pltpu.VMEM((PACK, 128), F32),
            pltpu.VMEM((4, PACK, 128), BF16),
            pltpu.VMEM((4, CHUNKS, ROWS, CHUNK), BF16),
            pltpu.VMEM((2, CHUNKS, HALF, CHUNK), BF16),
            pltpu.VMEM((2, CHUNKS, ROWS, CHUNK), BF16),
            pltpu.SemaphoreType.DMA((copies,)),
            pltpu.SemaphoreType.DMA((copies,)),
            pltpu.SemaphoreType.DMA((16,)),
        ],
        compiler_params=pltpu.CompilerParams(
            collective_id=0, has_side_effects=True, vmem_limit_bytes=62 << 20
        ),
    )(
        hid,
        weight,
        down,
        up,
        request_adapter.reshape(1, REQS),
        adapter_storage_slot.reshape(1, 128),
        cached_length_valid.reshape(1, REQS),
    )
    keys = cached_rotated_keys.reshape(REQS, 128, 128)
    values = cached_value_rows.reshape(REQS, 128, 128)
    return pl.pallas_call(
        attend,
        out_shape=jax.ShapeDtypeStruct((STEPS, REQS, 1024), BF16),
        grid_spec=pltpu.PrefetchScalarGridSpec(
            num_scalar_prefetch=1,
            grid=(REQS // BLOCK,),
            in_specs=[
                pl.BlockSpec((BLOCK * QROWS, 128), lambda i, n: (i, 0)),
                pl.BlockSpec((BLOCK * 8, 128), lambda i, n: (i, 0)),
                pl.BlockSpec((BLOCK * 8, 128), lambda i, n: (i, 0)),
                pl.BlockSpec((BLOCK, 128, 128), lambda i, n: (i, 0, 0)),
                pl.BlockSpec((BLOCK, 128, 128), lambda i, n: (i, 0, 0)),
            ],
            out_specs=pl.BlockSpec((STEPS, BLOCK, 1024), lambda i, n: (0, i, 0)),
            scratch_shapes=[
                pltpu.VMEM((BLOCK * QROWS, 128), F32),
                pltpu.VMEM((BLOCK * QROWS, 128), F32),
            ],
        ),
    )(cached_length_valid, query, key, value, keys, values)


def solution(mesh):
    placed = (
        P(None, "rep", "tp"),
        P(None, "tp", None),
        P("rep", "tp", None),
        P("rep", None, "tp", None),
        P("rep", "tp", None, None),
        P("rep", "tp", None, None),
        P("rep"),
        P("rep"),
        P(),
    )
    return jax.shard_map(
        local, mesh=mesh, in_specs=placed, out_specs=P(None, "rep", "tp"), check_vma=False
    )
```

```python
import functools

import jax
import jax.numpy as jnp
import numpy as np
from jax import lax
from jax.experimental import pallas as pl
from jax.experimental.pallas import tpu as pltpu
from jax.sharding import PartitionSpec as P

MESH = pl.DeviceIdType.MESH
F32 = jnp.float32
BF16 = jnp.bfloat16
STEPS = 3
REQS = 128
ROWS = STEPS * REQS
WIDTH = 1024
OUT = 1280
RANKS = 512
UP_PARTS = 4
UP_ROWS = RANKS // UP_PARTS
BLOCK = 32
BLOCKS = REQS // BLOCK
BROWS = STEPS * BLOCK
HALF = BROWS // 2
SUB = 16
PACK = ROWS // 2
PART = PACK // 8
PARTPAD = 32
QROWS = 24


def dot(a, b):
    return jnp.dot(a, b, preferred_element_type=F32)


def dot_nt(a, b):
    return lax.dot_general(a, b, (((1,), (1,)), ((), ())), preferred_element_type=F32)


def column(row):
    return jnp.transpose(jnp.broadcast_to(row, (128, 128)))


def verify(
    hid,
    weight,
    down,
    up,
    keys_in,
    values_in,
    req_ref,
    table_ref,
    len_ref,
    out,
    xs,
    rows,
    draw,
    wt,
    ups,
    wbuf,
    base,
    hits,
    spread,
    acc,
    reqs,
    slots,
    lengths,
    cosine,
    sine,
    home,
    home_in,
    part_in,
    low_part,
    low_parts,
    low_own,
    lows,
    low_both,
    dsend,
    relay_in,
    back_in,
    keys,
    values,
    query,
    new_key,
    new_value,
    mixed,
    ssem,
    rsem,
    lsem,
):
    rep = lax.axis_index("rep")
    tp = lax.axis_index("tp")
    x, z, y, c = rep // 4, rep % 4, tp // 2, tp % 2
    r = z * (1 - c) + x * c
    w = x * (1 - c) + z * c

    def rep_at(r_, w_):
        return (w_ * (1 - c) + r_ * c) * 4 + r_ * (1 - c) + w_ * c

    def dev(rep_, tp_):
        return {"rep": rep_, "tp": tp_}

    shift = (0, 3, 1, 2)
    row_reps = [rep_at((r + s) % 4, w) for s in shift]
    weight_reps = [rep_at(r, (w + s) % 4) for s in shift]
    row_dev = [dev(q, tp) for q in row_reps]
    weight_dev = [dev(q, tp) for q in weight_reps]
    tps = [((y + s) % 4) * 2 + c for s in shift]
    sib_tps = [((y + s) % 4) * 2 + 1 - c for s in shift]
    y_dev = [dev(rep, q) for q in tps]
    sibling = dev(rep, sib_tps[0])
    tp_dev = [dev(rep, (tp + k) % 8) for k in range(8)]

    count = [0]

    def remote(src, dst, device):
        i = count[0]
        count[0] += 1
        return pltpu.make_async_remote_copy(
            src_ref=src,
            dst_ref=dst,
            send_sem=ssem.at[i],
            recv_sem=rsem.at[i],
            device_id=device,
            device_id_type=MESH,
        )

    lcount = [0]

    def local(src, dst):
        i = lcount[0]
        lcount[0] += 1
        return pltpu.make_async_copy(src, dst, lsem.at[i])

    sent = []

    def go(*copies):
        for cp in copies:
            cp.start()
            sent.append(cp)

    class Ring:
        def __init__(self, src, slot, size, devs):
            a, b = (pl.ds(0, size // 2), pl.ds(size // 2, size // 2)) if size else (0, 1)
            left, right = devs[1], devs[2]
            self.first = [
                remote(src(a), slot(1, a), right),
                remote(src(b), slot(2, b), left),
            ]
            self.second = [
                remote(src(b), slot(1, b), right),
                remote(src(a), slot(2, a), left),
            ]
            self.far = [
                remote(slot(1, a), slot(3, a), right),
                remote(slot(2, b), slot(3, b), left),
            ]

        def relay(self):
            for i in range(2):
                self.first[i].wait_recv()
                go(self.far[i])

        def near(self):
            for i in range(2):
                self.second[i].wait_recv()

        def rest(self):
            for i in range(2):
                self.far[i].wait_recv()

    load_rows = local(hid, rows.at[0])
    load_down = local(down, draw)
    load_up = local(up, ups.at[0])
    order = ((0, 0), (0, 1), (1, 0), (2, 0), (1, 1), (2, 1), (3, 0), (3, 1))
    load_w = []
    for n, (i, s) in enumerate(order):
        t_ = (tps if s == 0 else sib_tps)[i]
        load_w.append(
            local(weight.at[pl.ds(pl.multiple_of(t_ * WIDTH, WIDTH), WIDTH), :], wbuf.at[n % 4])
        )
    load_keys = local(keys_in, keys)
    load_values = local(values_in, values)
    load_down.start()
    load_rows.start()
    load_w[0].start()
    load_w[1].start()

    reqs[0] = jnp.broadcast_to(req_ref[...], (8, 128))

    barrier = pltpu.get_barrier_semaphore()
    peers = [row_dev[1], row_dev[2], row_dev[3], weight_dev[1], weight_dev[2]] + tp_dev[1:]
    for peer in peers:
        pl.semaphore_signal(barrier, inc=1, device_id=peer, device_id_type=MESH)
    load_down.wait()
    for h in range(2):
        wt[0, h] = jnp.transpose(draw[h * 256 : (h + 1) * 256, :])
    pl.semaphore_wait(barrier, len(peers))

    y_ring = Ring(lambda h: hid.at[h], lambda s, h: xs.at[2 * s - 1, h], ROWS, y_dev)
    r_ring = Ring(lambda h: hid.at[h], lambda s, h: rows.at[s, h], ROWS, row_dev)
    w_ring = Ring(lambda h: wt.at[0, h], lambda s, h: wt.at[s, h], 0, weight_dev)
    up_rings = []
    for k in range(UP_PARTS):
        part = pl.ds(k * UP_ROWS, UP_ROWS)
        up_rings.append(
            Ring(
                lambda h, part=part: up.at[part, :].at[h],
                lambda s, h, part=part: ups.at[s, part, :].at[h],
                UP_ROWS,
                weight_dev,
            )
        )
    req_copies = [remote(reqs.at[0], reqs.at[(0, 2, 1, 3)[i]], row_dev[i]) for i in (1, 2, 3)]
    sib_copies = [remote(hid, xs.at[0], sibling)] + [
        remote(xs.at[2 * i - 1], xs.at[2 * i], sibling) for i in (1, 2, 3)
    ]

    go(*req_copies)
    go(*w_ring.first, *r_ring.first, *y_ring.first)
    go(*w_ring.second, *r_ring.second, *y_ring.second)
    go(sib_copies[0])
    load_w[2].start()
    load_w[3].start()
    load_up.start()
    load_keys.start()
    load_values.start()

    lane = lax.broadcasted_iota(jnp.int32, (128, 128), 1)
    low_lane = lane < 64

    freq = jnp.exp((lane % 64).astype(F32) * (-2.0 / 128) * jnp.log(F32(500000.0)))
    lengths[...] = column(len_ref[...])
    pos = lengths[...].astype(F32)
    for t in range(STEPS):
        angle = (pos + t) * freq
        part = pl.ds(t * REQS, REQS)
        cosine[part, :] = jnp.cos(angle)
        sine[part, :] = jnp.where(low_lane, -1.0, 1.0) * jnp.sin(angle)

    def rotate(v, at):
        return v * cosine[at, :] + pltpu.roll(v, 64, 1) * sine[at, :]

    def find_slots(i):
        hit = column(reqs[i, 0:1, :]) == lane
        found = jnp.sum(
            jnp.where(hit, jnp.broadcast_to(table_ref[...], (128, 128)), 0).astype(F32),
            axis=1,
            keepdims=True,
        )
        slots[i] = jnp.broadcast_to(found, (128, 128)).astype(jnp.int32)
        for j in range(4):
            for p in range(4):
                target = weight_reps[j] * 8 + 2 * p + jnp.where(low_lane, 0, 1)
                at = (j * 4 + p) * 128
                hits[i, :, at : at + 128] = jnp.where(slots[i] == target, 1.0, 0.0).astype(BF16)

    find_slots(0)

    done = [0]

    def base_mm(x_ref):
        n = done[0]
        done[0] += 1
        load_w[n].wait()
        got = dot(x_ref[...], wbuf[n % 4])
        if n == 0:
            base[...] = got
        else:
            base[...] += got
        if n + 4 < 8:
            load_w[n + 4].start()

    def down_mm(i, j, n=1):
        @pl.loop(0, 2)
        def _(h):
            got = dot(rows[i : i + n].reshape(n * ROWS, WIDTH), wt[j, h])
            for p in range(2):
                target = weight_reps[j] * 8 + h * 4 + 2 * p + jnp.where(low_lane, 0, 1)
                for q in range(n):
                    hit = slots[i + q] == target
                    for t in range(STEPS):
                        at = q * ROWS + t * REQS
                        acc[i + q, pl.ds(t * REQS, REQS), :] += jnp.where(
                            hit, got[at : at + REQS, p * 128 : (p + 1) * 128], 0.0
                        )

    acc[...] = jnp.zeros_like(acc)
    load_rows.wait()
    base_mm(rows.at[0])
    down_mm(0, 0)
    for cp in req_copies:
        cp.wait_recv()
    for i in (1, 2, 3):
        find_slots(i)
    sib_copies[0].wait_recv()
    base_mm(xs.at[0])

    y_ring.relay()
    r_ring.relay()
    w_ring.relay()
    for ring in up_rings:
        go(*ring.first, *ring.second)

    y_ring.near()
    go(sib_copies[1], sib_copies[2])
    r_ring.near()
    down_mm(1, 0, 2)
    base_mm(xs.at[1])
    w_ring.near()
    down_mm(0, 1, 3)
    down_mm(0, 2, 3)
    base_mm(xs.at[3])
    y_ring.rest()
    go(sib_copies[3])
    r_ring.rest()
    for j in (0, 1, 2):
        down_mm(3, j)
    w_ring.rest()

    home_copies = []
    lane_h = lax.broadcasted_iota(jnp.int32, (PACK, 128), 1) < 64
    for i in (3, 1, 2, 0):
        down_mm(i, 3)
        both = acc[i] + pltpu.roll(acc[i], 64, 1)
        home[i] = jnp.where(lane_h, both[:PACK], both[PACK:])
        if i:
            cp = remote(home.at[i], home_in.at[(0, 2, 1, 3)[i]], row_dev[i])
            home_copies.append(cp)
            go(cp)
    up_rings[0].relay()
    sib_copies[1].wait_recv()
    base_mm(xs.at[2])
    for cp in home_copies:
        cp.wait_recv()
    home[0] = (home[0] + home_in[1]) + (home_in[2] + home_in[3])
    part_copies = []
    for k in range(1, 8):
        target = (tp + k) % 8
        cp = remote(
            home.at[0, pl.ds(pl.multiple_of(target * PART, 8), PART), :], part_in.at[k], tp_dev[k]
        )
        part_copies.append(cp)
        go(cp)
    up_rings[1].relay()
    sib_copies[2].wait_recv()
    base_mm(xs.at[4])
    for cp in part_copies:
        cp.wait_recv()
    total = home[0, pl.ds(pl.multiple_of(tp * PART, 8), PART), :]
    for k in range(1, 8):
        total = total + part_in[k]
    low_part[...] = jnp.concatenate([total, jnp.zeros((PARTPAD - PART, 128), F32)], 0).astype(BF16)
    low_copies = []
    for k in range(1, 8):
        cp = remote(low_part, low_parts.at[k], tp_dev[k])
        low_copies.append(cp)
        go(cp)
    up_rings[2].relay()
    base_mm(xs.at[5])
    for cp in low_copies:
        cp.wait_recv()
    low_own[pl.ds(pl.multiple_of(tp * PART, 8), PART), :] = low_part[...].astype(F32)[:PART]
    for k in range(1, 8):
        source = (tp + 8 - k) % 8
        low_own[pl.ds(pl.multiple_of(source * PART, 8), PART), :] = low_parts[k].astype(F32)[:PART]
    lows[0] = low_own[...].astype(BF16)
    back_low = [remote(lows.at[0], lows.at[(0, 2, 1, 3)[i]], row_dev[i]) for i in (1, 2, 3)]
    go(*back_low)

    def unpack(i):
        packed = lows[i].astype(F32)
        turned = pltpu.roll(packed, 64, 1)
        low_both[i, :PACK, :] = jnp.where(lane_h, packed, turned).astype(BF16)
        low_both[i, PACK:, :] = jnp.where(lane_h, turned, packed).astype(BF16)

    unpack(0)
    up_rings[3].relay()
    sib_copies[3].wait_recv()
    base_mm(xs.at[6])
    for cp in back_low:
        cp.wait_recv()
    for i in (1, 2, 3):
        unpack(i)
    load_up.wait()
    for ring in up_rings:
        ring.near()
        ring.rest()

    ha, hb = pl.ds(0, HALF), pl.ds(HALF, HALF)
    far_back, near_back, late_back = {}, {}, {}

    def send_block(b):
        for i in range(4):
            for t in range(STEPS):
                low = low_both[i, t * REQS + b * BLOCK : t * REQS + (b + 1) * BLOCK, :]
                at = i * BROWS + t * BLOCK
                for n in range(16):
                    spread[at : at + BLOCK, n * 128 : (n + 1) * 128] = (
                        hits[i, b * BLOCK : (b + 1) * BLOCK, n * 128 : (n + 1) * 128] * low
                    )
        got = dot(spread[...], ups[...].reshape(4 * RANKS, OUT)).astype(BF16)
        for i in range(4):
            dsend[b, i] = got[i * BROWS : (i + 1) * BROWS]
        far_back[b] = [
            remote(dsend.at[b, 3, ha], relay_in.at[0, b], row_dev[2]),
            remote(dsend.at[b, 3, hb], relay_in.at[1, b], row_dev[1]),
        ]
        near_back[b] = [
            remote(dsend.at[b, 2, hb], back_in.at[0, b, hb], row_dev[2]),
            remote(dsend.at[b, 1, ha], back_in.at[1, b, ha], row_dev[1]),
        ]
        go(*far_back[b], *near_back[b])

    def relay_block(b):
        far_back[b][0].wait_recv()
        dsend[b, 2, ha, :] = dsend[b, 2, ha, :] + relay_in[0, b]
        far_back[b][1].wait_recv()
        dsend[b, 1, hb, :] = dsend[b, 1, hb, :] + relay_in[1, b]
        late_back[b] = [
            remote(dsend.at[b, 2, ha], back_in.at[0, b, ha], row_dev[2]),
            remote(dsend.at[b, 1, hb], back_in.at[1, b, hb], row_dev[1]),
        ]
        go(*late_back[b])

    factor = 128**-0.5

    def attend(b, s):
        first = b * BLOCK + s * SUB
        n_rows = SUB * QROWS
        q = query[pl.ds(pl.multiple_of(s * n_rows, 8), n_rows), :].astype(BF16)
        fresh_at = pl.ds(pl.multiple_of(s * SUB * 8, 8), SUB * 8)
        row = lax.broadcasted_iota(jnp.int32, (n_rows, 128), 0)
        col = lax.broadcasted_iota(jnp.int32, (n_rows, 128), 1)
        open_ = (row // QROWS == col // 8) & (col % 8 <= (row % QROWS) // 8)
        fresh = dot_nt(q, new_key[fresh_at, :].astype(BF16)) * factor
        fresh = jnp.where(open_, fresh, -jnp.inf)
        lane_q = lax.broadcasted_iota(jnp.int32, (QROWS, 128), 1)
        parts = []
        for i in range(SUB // 2):
            pair = keys[pl.ds(first + 2 * i, 2)].reshape(256, 128)
            got = dot_nt(q[2 * i * QROWS : (2 * i + 2) * QROWS], pair) * factor
            for k in range(2):
                length = jnp.broadcast_to(lengths[pl.ds(first + 2 * i + k, 1), :], (QROWS, 128))
                parts.append(
                    jnp.where(
                        lane_q < length,
                        got[k * QROWS : (k + 1) * QROWS, k * 128 : (k + 1) * 128],
                        -jnp.inf,
                    )
                )
        cached = jnp.concatenate(parts, 0)
        highest = jnp.max(jnp.maximum(cached, fresh), axis=1, keepdims=True)
        cached = jnp.exp(cached - highest)
        fresh = jnp.exp(fresh - highest)
        scale = 1.0 / jnp.sum(cached + fresh, axis=1, keepdims=True)
        cached = (cached * scale).astype(BF16)
        fresh = (fresh * scale).astype(BF16)
        extra = dot(fresh, new_value[fresh_at, :].astype(BF16))
        for i in range(SUB):
            at = i * QROWS
            mixed[at : at + QROWS, :] = extra[at : at + QROWS] + dot(
                cached[at : at + QROWS], values[first + i]
            )
        for t in range(STEPS):
            for g in range(8):
                out[t, pl.ds(pl.multiple_of(first, SUB), SUB), g * 128 : (g + 1) * 128] = mixed[
                    pl.ds(t * 8 + g, SUB, stride=QROWS), :
                ].astype(BF16)

    def finish_block(b):
        for cp in near_back[b] + late_back[b]:
            cp.wait_recv()
        for t in range(STEPS):
            at = slice(t * BLOCK, (t + 1) * BLOCK)
            whole = slice(t * REQS + b * BLOCK, t * REQS + (b + 1) * BLOCK)
            add = (dsend[b, 0, at, :].astype(F32) + back_in[0, b, at, :].astype(F32)) + back_in[
                1, b, at, :
            ].astype(F32)
            joined = base[whole, :] + add
            for g in range(8):
                query[pl.ds(t * 8 + g, BLOCK, stride=QROWS), :] = rotate(
                    joined[:, g * 128 : (g + 1) * 128], whole
                )
            new_key[pl.ds(t, BLOCK, stride=8), :] = rotate(joined[:, 1024:1152], whole)
            new_value[pl.ds(t, BLOCK, stride=8), :] = joined[:, 1152:]

        @pl.loop(0, BLOCK // SUB)
        def _(s):
            attend(b, s)

    new_key[...] = jnp.zeros_like(new_key)
    new_value[...] = jnp.zeros_like(new_value)
    send_block(0)
    send_block(1)
    relay_block(0)
    send_block(2)
    relay_block(1)
    send_block(3)
    relay_block(2)
    load_keys.wait()
    load_values.wait()
    finish_block(0)
    relay_block(3)
    finish_block(1)
    finish_block(2)
    finish_block(3)
    for cp in sent:
        cp.wait_send()


def local(
    normed_hidden_input,
    query_key_value_weight,
    adapter_down_weight,
    adapter_up_weight,
    cached_rotated_keys,
    cached_value_rows,
    cached_length_valid,
    request_adapter,
    adapter_storage_slot,
):
    hid = normed_hidden_input.reshape(ROWS, WIDTH)
    weight = query_key_value_weight.reshape(8 * WIDTH, OUT)
    down = jnp.swapaxes(adapter_down_weight, 1, 2).reshape(RANKS, WIDTH)
    up = adapter_up_weight.reshape(RANKS, OUT)
    anywhere = pl.BlockSpec(memory_space=pl.ANY)
    in_vmem = pl.BlockSpec(memory_space=pltpu.VMEM)
    copies = 140
    return pl.pallas_call(
        verify,
        out_shape=jax.ShapeDtypeStruct((STEPS, REQS, 1024), BF16),
        in_specs=[anywhere] * 6 + [in_vmem] * 3,
        out_specs=in_vmem,
        scratch_shapes=[
            pltpu.VMEM((7, ROWS, WIDTH), BF16),
            pltpu.VMEM((4, ROWS, WIDTH), BF16),
            pltpu.VMEM((RANKS, WIDTH), BF16),
            pltpu.VMEM((4, 2, WIDTH, 256), BF16),
            pltpu.VMEM((4, RANKS, OUT), BF16),
            pltpu.VMEM((4, WIDTH, OUT), BF16),
            pltpu.VMEM((ROWS, OUT), F32),
            pltpu.VMEM((4, REQS, 4 * RANKS), BF16),
            pltpu.VMEM((4 * BROWS, 4 * RANKS), BF16),
            pltpu.VMEM((4, ROWS, 128), F32),
            pltpu.VMEM((4, 8, 128), jnp.int32),
            pltpu.VMEM((4, 128, 128), jnp.int32),
            pltpu.VMEM((REQS, 128), jnp.int32),
            pltpu.VMEM((ROWS, 128), F32),
            pltpu.VMEM((ROWS, 128), F32),
            pltpu.VMEM((4, PACK, 128), F32),
            pltpu.VMEM((4, PACK, 128), F32),
            pltpu.VMEM((8, PART, 128), F32),
            pltpu.VMEM((PARTPAD, 128), BF16),
            pltpu.VMEM((8, PARTPAD, 128), BF16),
            pltpu.VMEM((PACK, 128), F32),
            pltpu.VMEM((4, PACK, 128), BF16),
            pltpu.VMEM((4, ROWS, 128), BF16),
            pltpu.VMEM((BLOCKS, 4, BROWS, OUT), BF16),
            pltpu.VMEM((2, BLOCKS, HALF, OUT), BF16),
            pltpu.VMEM((2, BLOCKS, BROWS, OUT), BF16),
            pltpu.VMEM((REQS, 128, 128), BF16),
            pltpu.VMEM((REQS, 128, 128), BF16),
            pltpu.VMEM((BLOCK * QROWS, 128), F32),
            pltpu.VMEM((BLOCK * 8, 128), F32),
            pltpu.VMEM((BLOCK * 8, 128), F32),
            pltpu.VMEM((SUB * QROWS, 128), F32),
            pltpu.SemaphoreType.DMA((copies,)),
            pltpu.SemaphoreType.DMA((copies,)),
            pltpu.SemaphoreType.DMA((16,)),
        ],
        compiler_params=pltpu.CompilerParams(
            collective_id=0, has_side_effects=True, vmem_limit_bytes=62 << 20
        ),
    )(
        hid,
        weight,
        down,
        up,
        cached_rotated_keys.reshape(REQS, 128, 128),
        cached_value_rows.reshape(REQS, 128, 128),
        request_adapter.reshape(1, REQS),
        adapter_storage_slot.reshape(1, 128),
        cached_length_valid.reshape(1, REQS),
    )


def solution(mesh):
    placed = (
        P(None, "rep", "tp"),
        P(None, "tp", None),
        P("rep", "tp", None),
        P("rep", None, "tp", None),
        P("rep", "tp", None, None),
        P("rep", "tp", None, None),
        P("rep"),
        P("rep"),
        P(),
    )
    return jax.shard_map(
        local, mesh=mesh, in_specs=placed, out_specs=P(None, "rep", "tp"), check_vma=False
    )
```
